32 devices in a mesh: energy: 2 (over x), strip: 16 (over z, y, core).
Axes of the slice: x: 2, y: 2, z: 4, core: 2. Of those that a mesh axis runs over, the one named last changes fastest.
Arguments:
- object_field: float32 [64, 2, 1024, 384], P('energy', None, 'strip'), may hold values from -5 to 5
- probe_modes: float32 [64, 3, 2, 128, 128], P('energy'), may hold values from -2.5 to 2.5
- measured: float32 [64, 16, 5, 128, 128], P('energy', 'strip'), may hold values from 0.5 to 3
- scan_cols: int32 [16, 5], replicated, may hold values from 0 to 256, as said below
- spectra: float32 [64, 2, 8], replicated, may hold values from -4 to 4
- material_order: int32 [8], replicated, may hold values from 0 to 7, each once
Outputs:
- refined_object: float32 [64, 2, 1024, 384], P('energy', None, 'strip')
- abundance: float32 [8, 2, 16, 64, 384], P(None, None, 'strip', 'energy')
The draws below stay inside these ranges and needn't reach their ends.
Inputs may be any that keep to these rules, and one draw needn't show every extreme that they name: `scan_cols`: row b lists the first columns of the scan positions of band b, whose top row is b * 64; they rise, neighbours differ by 32 to 96, the first is 0 and the last 256. `material_order`: each material once.
All inputs are finite; a program needn't handle non-finite values.
Results may differ from the reference program's by a relative error of at most 0.0013.
Values sent between devices are 32-bit elements; how exact they have to be, the bound alone decides.
A program may use at most 128 MiB of HBM per device.

```python
import jax
import jax.numpy as jnp
from jax import lax

PSIZE = 128
MODES = 3
MATS = 8
ENERGIES = 64
STEP = 64
COLS = 384
OUTER = 1
INNER = 1
BANDS = 16
ROWS = 1024
POS = 5


def draw_scan_cols(key, part):
    base_cols = jnp.arange(POS, dtype=jnp.int32) * STEP
    jitter = jax.random.randint(jax.random.fold_in(key, 11), (BANDS, POS), -(STEP // 4), STEP // 4 + 1, dtype=jnp.int32)
    offsets = jnp.clip(base_cols[None, :] + jitter, 0, COLS - PSIZE)
    offsets = offsets.at[:, 0].set(0)
    offsets = offsets.at[:, POS - 1].set(COLS - PSIZE)
    return offsets.astype(jnp.int32)


def levels(rng, shape, cuts, least, largest):
    def one(dim, parts):
        steps = jax.random.uniform(jax.random.fold_in(jax.random.fold_in(rng, 6), dim), (parts,), jnp.float32, least / len(cuts), largest / len(cuts))
        return jnp.repeat(jnp.exp(steps), shape[dim] // parts).reshape((-1,) + (1,) * (len(shape) - dim - 1))

    level = one(*cuts[0])
    for cut in cuts[1:]:
        level = level * one(*cut)
    return level


def normal_values(stream_key, shape, width, reach, shards=(), held_as=jnp.bfloat16):
    factor_of = levels(stream_key, shape, shards, -0.22, 0.18) if shards else 1.0
    entries = jax.random.normal(stream_key, shape, jnp.float32) * width * factor_of
    return jnp.minimum(jnp.maximum(entries, -reach), reach).astype(held_as)


def setup_inputs(seed: int = 0) -> dict:
    splits = jax.random.split(jax.random.key(seed), 7)
    return {
        "object_field": normal_values(splits[0], (ENERGIES, 2, ROWS, COLS), 1.0, 5.0, ((0, 2), (2, 16)), jnp.float32),
        "probe_modes": normal_values(splits[1], (ENERGIES, MODES, 2, PSIZE, PSIZE), 0.5, 2.5, ((0, 2),), jnp.float32),
        "measured": jnp.clip(0.5 + 2.5 * jax.random.uniform(splits[2], (ENERGIES, BANDS, POS, PSIZE, PSIZE), jnp.float32) ** levels(splits[2], (ENERGIES, BANDS, POS, PSIZE, PSIZE), ((0, 2), (1, 16)), -0.2, 0.2), 0.5, 3.0),
        "scan_cols": draw_scan_cols(jax.random.fold_in(splits[6], 71), 0),
        "spectra": normal_values(splits[4], (ENERGIES, 2, MATS), 1.0, 4.0, (), jnp.float32),
        "material_order": jax.random.permutation(splits[5], MATS).astype(jnp.int32),
    }


PRECISE = lax.Precision.HIGHEST

def dft_tables(probe_width, phase_sign):
    counter = jnp.arange(probe_width, dtype=jnp.int32)
    phase_index = counter[:, None] * counter[None, :] % probe_width
    angle_grid = phase_index.astype(jnp.float32) * (2.0 * jnp.pi / probe_width)
    root_width = jnp.sqrt(jnp.float32(probe_width))
    cosine_table = (jnp.cos(angle_grid) / root_width).astype(jnp.bfloat16)
    sine_table = (phase_sign * jnp.sin(angle_grid) / root_width).astype(jnp.bfloat16)
    blocks = jnp.stack([jnp.stack([cosine_table, sine_table]), jnp.stack([-sine_table, cosine_table])])
    return (blocks.transpose(0, 2, 1, 3), blocks.transpose(1, 2, 0, 3))

def transform(left_table, right_table, waves):
    first_section = jnp.einsum('dacj,emcjb->emdab', left_table.astype(jnp.float32), waves.astype(jnp.float32), precision=PRECISE)
    first_section = lax.optimization_barrier(first_section.astype(jnp.bfloat16))
    return jnp.einsum('emcab,cbdk->emdak', first_section.astype(jnp.float32), right_table.astype(jnp.float32), precision=PRECISE)

def band_gradient(window, measured_band, band_cols, probe_modes, tables):
    forward_left, forward_right, inverse_left, inverse_right = tables
    probe_real = probe_modes[:, :, 0]
    probe_imag = probe_modes[:, :, 1]

    def accumulate(position, gradient_total):
        column = lax.dynamic_index_in_dim(band_cols, position, 0, keepdims=False)
        measured_point = lax.dynamic_index_in_dim(measured_band, position, 1, keepdims=False)
        object_patch = lax.dynamic_slice_in_dim(window, column, PSIZE, axis=3)
        object_real = object_patch[:, None, 0]
        object_imag = object_patch[:, None, 1]
        exit_wave = jnp.stack([probe_real * object_real - probe_imag * object_imag, probe_real * object_imag + probe_imag * object_real], axis=2)
        exit_wave = lax.optimization_barrier(exit_wave.astype(jnp.bfloat16))
        spectrum = transform(forward_left, forward_right, exit_wave)
        intensity = lax.optimization_barrier(jnp.sum(spectrum * spectrum, axis=(1, 2)))
        scaling = measured_point / jnp.sqrt(jnp.maximum(intensity, 0.25))
        corrected = lax.optimization_barrier((spectrum * scaling[:, None, None]).astype(jnp.bfloat16))
        returned = transform(inverse_left, inverse_right, corrected)
        residual_wave = exit_wave.astype(jnp.float32) - returned
        wave_real = residual_wave[:, :, 0]
        wave_imag = residual_wave[:, :, 1]
        grad_real = lax.optimization_barrier(jnp.sum(probe_real * wave_real + probe_imag * wave_imag, axis=1))
        grad_imag = lax.optimization_barrier(jnp.sum(probe_real * wave_imag - probe_imag * wave_real, axis=1))
        update = jnp.stack([grad_real, grad_imag], axis=1)
        current = lax.dynamic_slice_in_dim(gradient_total, column, PSIZE, axis=3)
        return lax.dynamic_update_slice_in_dim(gradient_total, current + update, column, axis=3)
    return lax.fori_loop(0, POS, accumulate, jnp.zeros_like(window))

def descent_pass(estimate, measured, scan_cols, probe_modes, tables, step_size):
    padded = jnp.pad(estimate, ((0, 0), (0, 0), (0, STEP), (0, 0)))

    def band_step(gradient_sum, band_index):
        first_row = band_index * STEP
        window = lax.dynamic_slice_in_dim(padded, first_row, PSIZE, axis=2)
        measured_band = lax.dynamic_index_in_dim(measured, band_index, 1, keepdims=False)
        band_cols = lax.dynamic_index_in_dim(scan_cols, band_index, 0, keepdims=False)
        gradient = band_gradient(window, measured_band, band_cols, probe_modes, tables)
        current = lax.dynamic_slice_in_dim(gradient_sum, first_row, PSIZE, axis=2)
        return (lax.dynamic_update_slice_in_dim(gradient_sum, current + gradient, first_row, axis=2), None)
    gradient_sum, _ = lax.scan(band_step, jnp.zeros_like(padded), jnp.arange(BANDS, dtype=jnp.int32))
    return estimate - step_size[:, None, None, None] * gradient_sum[:, :, :ROWS]

def build_basis(spectra):
    spectra_real = spectra[:, 0]
    spectra_imag = spectra[:, 1]
    upper_rows = jnp.stack([spectra_real, -spectra_imag], axis=-1)
    lower_rows = jnp.stack([spectra_imag, spectra_real], axis=-1)
    return jnp.stack([upper_rows, lower_rows], axis=1).reshape(2 * ENERGIES, 2 * MATS)

def reference(object_field, probe_modes, measured, scan_cols, spectra, material_order):
    forward_left, forward_right = dft_tables(PSIZE, 1)
    inverse_left, inverse_right = dft_tables(PSIZE, -1)
    tables = (forward_left, forward_right, inverse_left, inverse_right)
    probe_power = lax.optimization_barrier(jnp.sum(probe_modes * probe_modes, axis=(1, 2)))
    step_size = 0.5 / lax.optimization_barrier(jnp.max(probe_power, axis=(1, 2)))
    basis_matrix = build_basis(spectra)
    gram_matrix = jnp.dot(basis_matrix.T, basis_matrix, precision=PRECISE)
    solver_map = jnp.linalg.solve(gram_matrix, basis_matrix.T)
    estimate = object_field
    coefficients = jnp.zeros((2 * MATS, ROWS * COLS), jnp.float32)
    for outer_step in range(OUTER):
        for inner_step in range(INNER):
            estimate = descent_pass(estimate, measured, scan_cols, probe_modes, tables, step_size)
        spectra_rows = estimate.reshape(2 * ENERGIES, ROWS * COLS)
        coefficients = jnp.dot(solver_map, spectra_rows, precision=PRECISE)
        estimate = jnp.dot(basis_matrix, coefficients, precision=PRECISE).reshape(ENERGIES, 2, ROWS, COLS)
    abundance = coefficients.reshape(MATS, 2, BANDS, STEP, COLS)
    abundance = jnp.take(abundance, material_order, axis=0)
    return (estimate, abundance)
```

```python
import functools

import jax
import jax.numpy as jnp
import ml_dtypes
import numpy as np
from jax import lax
from jax.experimental import pallas as pl
from jax.experimental.pallas import tpu as pltpu
from jax.sharding import PartitionSpec as P

PRECISE = lax.Precision.HIGHEST
CHUNKS = 4
LANES = 128


def shifted(block, axis, distance):
    devices = range(lax.axis_size(axis))
    route = [(i - distance, i) for i in devices if i - distance in devices]
    return lax.ppermute(block, axis, route)


def dft_tables(width, phase_sign):
    counter = np.arange(width)
    angle = (counter[:, None] * counter[None, :] % width) * (2.0 * np.pi / width)
    cosine = (np.cos(angle) / np.sqrt(width)).astype(ml_dtypes.bfloat16)
    sine = (phase_sign * np.sin(angle) / np.sqrt(width)).astype(ml_dtypes.bfloat16)
    left = np.block([[cosine, sine], [-sine, cosine]])
    right = np.block([[cosine, -sine], [sine, cosine]])
    return jnp.asarray(left), jnp.asarray(right)


def gradient_kernel(
    cols, own, halo, probe, measured, fl, fr, il, ir, upper, lower, window, grad
):
    modes, _, width, _ = probe.shape[1:]
    positions = measured.shape[2]
    rows, columns = own.shape[2:]
    f32, bf16 = jnp.float32, jnp.bfloat16
    lane = lax.broadcasted_iota(jnp.int32, (width, width), 1)
    window[:, :rows, :columns] = own[0]
    window[:, rows:, :columns] = halo[0]
    window[:, :, columns:] = jnp.zeros((2, width, width), f32)
    grad[...] = jnp.zeros(grad.shape, f32)
    power = jnp.zeros((width, width), f32)
    for m in range(modes):
        power += probe[0, m, 0] * probe[0, m, 0] + probe[0, m, 1] * probe[0, m, 1]
    step = 0.5 / jnp.max(jnp.max(power, axis=0, keepdims=True), axis=1, keepdims=True)

    def product(left, right, x):
        y = jnp.dot(left, x, preferred_element_type=f32).astype(bf16)
        y = jnp.concatenate(
            [
                jnp.concatenate(
                    [y[:width, m * width : (m + 1) * width], y[width:, m * width : (m + 1) * width]],
                    axis=1,
                )
                for m in range(modes)
            ],
            axis=0,
        )
        s = jnp.dot(y, right, preferred_element_type=f32)
        return [
            (s[m * width : (m + 1) * width, :width], s[m * width : (m + 1) * width, width:])
            for m in range(modes)
        ]

    def stacked(pairs):
        return jnp.concatenate(
            [jnp.concatenate([re, im], axis=0) for re, im in pairs], axis=1
        )

    for p in range(positions):
        col = cols[p]
        off = col % width
        base = pl.multiple_of(col - off, LANES)
        back = (width - off) % width
        first, second = pl.ds(base, width), pl.ds(base + width, width)

        def patch(c):
            a = pltpu.roll(window[c, :, first], back, 1)
            b = pltpu.roll(window[c, :, second], back, 1)
            return jnp.where(lane < width - off, a, b)

        o_re, o_im = patch(0), patch(1)
        waves = []
        for m in range(modes):
            p_re, p_im = probe[0, m, 0], probe[0, m, 1]
            waves.append(
                (
                    (p_re * o_re - p_im * o_im).astype(bf16),
                    (p_re * o_im + p_im * o_re).astype(bf16),
                )
            )
        spectrum = product(fl[...], fr[...], stacked(waves))
        intensity = sum(re * re + im * im for re, im in spectrum)
        scale = measured[0, 0, p] * lax.rsqrt(jnp.maximum(intensity, 0.25))
        corrected = [((re * scale).astype(bf16), (im * scale).astype(bf16)) for re, im in spectrum]
        returned = product(il[...], ir[...], stacked(corrected))
        g_re = jnp.zeros((width, width), f32)
        g_im = jnp.zeros((width, width), f32)
        for m in range(modes):
            p_re, p_im = probe[0, m, 0], probe[0, m, 1]
            w_re = waves[m][0].astype(f32) - returned[m][0]
            w_im = waves[m][1].astype(f32) - returned[m][1]
            g_re += p_re * w_re + p_im * w_im
            g_im += p_re * w_im - p_im * w_re
        for c, g in ((0, g_re), (1, g_im)):
            turned = pltpu.roll(g, off, 1)
            grad[c, :, first] += jnp.where(lane >= off, turned, 0.0)
            grad[c, :, second] += jnp.where(lane < off, turned, 0.0)
    for c in range(2):
        upper[0, c] = own[0, c] - step * grad[c, :rows, :columns]
        lower[0, c] = -step * grad[c, rows:, :columns]


def chunk_gradient(cols, object_field, halo, probe, measured, tables, start):
    count = halo.shape[0]
    energies, _, rows, columns = object_field.shape
    modes, _, width, _ = probe.shape[1:]
    positions = measured.shape[2]
    field = jax.ShapeDtypeStruct((count, 2, rows, columns), jnp.float32)
    table = pl.BlockSpec((2 * width, 2 * width), lambda e, c: (0, 0))
    piece = pl.BlockSpec((1, 2, rows, columns), lambda e, c: (e, 0, 0, 0))
    flops = 4 * 2 * (2 * width) * (2 * width) * width * modes * positions * count
    return pl.pallas_call(
        gradient_kernel,
        grid_spec=pltpu.PrefetchScalarGridSpec(
            num_scalar_prefetch=1,
            grid=(count,),
            in_specs=[
                pl.BlockSpec((1, 2, rows, columns), lambda e, c: (e + start, 0, 0, 0)),
                piece,
                pl.BlockSpec((1, modes, 2, width, width), lambda e, c: (e + start, 0, 0, 0, 0)),
                pl.BlockSpec(
                    (1, 1, positions, width, width), lambda e, c: (e + start, 0, 0, 0, 0)
                ),
                table,
                table,
                table,
                table,
            ],
            out_specs=[piece, piece],
            scratch_shapes=[
                pltpu.VMEM((2, width, columns + width), jnp.float32),
                pltpu.VMEM((2, width, columns + width), jnp.float32),
            ],
        ),
        out_shape=[field, field],
        compiler_params=pltpu.CompilerParams(
            dimension_semantics=("arbitrary",), vmem_limit_bytes=40 * 2**20
        ),
        cost_estimate=pl.CostEstimate(
            flops=3 * flops, bytes_accessed=count * 1800000, transcendentals=0
        ),
    )(cols, object_field, halo, probe, measured, *tables)


def solver_kernel(gram, rhs, out):
    size = gram.shape[0]
    g, b = gram[...], rhs[...]
    row = lax.broadcasted_iota(jnp.int32, (size, 1), 0)
    for k in range(size):
        inverse = 1.0 / g[k : k + 1, k : k + 1]
        g_row, b_row = g[k : k + 1] * inverse, b[k : k + 1] * inverse
        column = g[:, k : k + 1]
        g = jnp.where(row == k, g_row, g - column * g_row)
        b = jnp.where(row == k, b_row, b - column * b_row)
    out[...] = b


def build_basis(spectra):
    re, im = spectra[:, 0], spectra[:, 1]
    upper = jnp.stack([re, -im], axis=-1)
    lower = jnp.stack([im, re], axis=-1)
    return jnp.stack([upper, lower], axis=1).reshape(2 * spectra.shape[0], 2 * spectra.shape[2])


def on_device(object_field, probe_modes, measured, scan_cols, spectra, material_order):
    width = probe_modes.shape[-1]
    energies, _, rows, columns = object_field.shape
    materials = spectra.shape[2]
    chunk = energies // CHUNKS if energies % CHUNKS == 0 else energies
    starts = range(0, energies, chunk)
    halos = [shifted(object_field[s : s + chunk], "strip", -1) for s in starts]
    strip_index = lax.axis_index("strip")
    energy_index = lax.axis_index("energy")
    cols = lax.dynamic_index_in_dim(scan_cols, strip_index, 0, keepdims=False)
    tables = (*dft_tables(width, 1), *dft_tables(width, -1))
    basis = build_basis(spectra)
    gram = jnp.dot(basis.T, basis, precision=PRECISE)
    solver_map = pl.pallas_call(
        solver_kernel, out_shape=jax.ShapeDtypeStruct(basis.T.shape, jnp.float32)
    )(gram, basis.T)
    first = energy_index * (2 * energies)
    own_map = lax.dynamic_slice_in_dim(solver_map, first, 2 * energies, axis=1)
    own_basis = lax.dynamic_slice_in_dim(basis, first, 2 * energies, axis=0)
    kept, carried = 0.0, 0.0
    for s, halo in zip(starts, halos):
        upper, lower = chunk_gradient(cols, object_field, halo, probe_modes, measured, tables, s)
        part = own_map[:, 2 * s : 2 * (s + chunk)].reshape(2 * materials, chunk, 2)
        product = functools.partial(jnp.einsum, "kec,ecrx->krx", precision=PRECISE)
        kept += product(part, upper)
        carried += product(part, lower)
    coefficients = lax.psum(kept + shifted(carried, "strip", 1), "energy")
    estimate = jnp.einsum(
        "eck,krx->ecrx",
        own_basis.reshape(energies, 2, 2 * materials),
        coefficients,
        precision=PRECISE,
    )
    sub_rows = rows // lax.axis_size("energy")
    half = lax.dynamic_slice_in_dim(coefficients, energy_index * sub_rows, sub_rows, axis=1)
    half = half.reshape(materials, 2, 1, sub_rows, columns)
    abundance = jnp.concatenate(
        [
            lax.dynamic_index_in_dim(half, material_order[k], 0, keepdims=True)
            for k in range(materials)
        ],
        axis=0,
    )
    return (estimate, abundance)


def solution(mesh):
    return jax.shard_map(
        on_device,
        mesh=mesh,
        in_specs=(
            P("energy", None, "strip", None),
            P("energy", None, None, None, None),
            P("energy", "strip", None, None, None),
            P(),
            P(),
            P(),
        ),
        out_specs=(P("energy", None, "strip", None), P(None, None, "strip", "energy", None)),
        check_vma=False,
    )
```

```python
import functools

import jax
import jax.numpy as jnp
import ml_dtypes
import numpy as np
from jax import lax
from jax.experimental import pallas as pl
from jax.experimental.pallas import tpu as pltpu
from jax.sharding import PartitionSpec as P

PRECISE = lax.Precision.HIGHEST
CHUNKS = 4
LANES = 128


def shifted(block, axis, distance):
    devices = range(lax.axis_size(axis))
    route = [(i - distance, i) for i in devices if i - distance in devices]
    return lax.ppermute(block, axis, route)


def dft_tables(width, phase_sign):
    counter = np.arange(width)
    angle = (counter[:, None] * counter[None, :] % width) * (2.0 * np.pi / width)
    cosine = (np.cos(angle) / np.sqrt(width)).astype(ml_dtypes.bfloat16)
    sine = (phase_sign * np.sin(angle) / np.sqrt(width)).astype(ml_dtypes.bfloat16)
    left = np.block([[cosine, sine], [-sine, cosine]])
    right = np.block([[cosine, -sine], [sine, cosine]])
    return jnp.asarray(left), jnp.asarray(right)


def gradient_kernel(
    cols, own, halo, probe, measured, fl, fr, il, ir, upper, lower, window, grad
):
    modes, _, width, _ = probe.shape[1:]
    positions = measured.shape[2]
    rows, columns = own.shape[2:]
    f32, bf16 = jnp.float32, jnp.bfloat16
    lane = lax.broadcasted_iota(jnp.int32, (width, width), 1)
    window[:, :rows, :columns] = own[0]
    window[:, rows:, :columns] = halo[0]
    window[:, :, columns:] = jnp.zeros((2, width, width), f32)
    grad[...] = jnp.zeros(grad.shape, f32)
    power = jnp.zeros((width, width), f32)
    for m in range(modes):
        power += probe[0, m, 0] * probe[0, m, 0] + probe[0, m, 1] * probe[0, m, 1]
    step = 0.5 / jnp.max(jnp.max(power, axis=0, keepdims=True), axis=1, keepdims=True)

    def first_product(left, x):
        y = jnp.dot(left, x, preferred_element_type=f32).astype(bf16)
        return jnp.concatenate(
            [
                jnp.concatenate(
                    [y[:width, m * width : (m + 1) * width], y[width:, m * width : (m + 1) * width]],
                    axis=1,
                )
                for m in range(modes)
            ],
            axis=0,
        )

    def second_product(y, right):
        s = jnp.dot(y, right, preferred_element_type=f32)
        return [
            (s[m * width : (m + 1) * width, :width], s[m * width : (m + 1) * width, width:])
            for m in range(modes)
        ]

    def stacked(pairs):
        return jnp.concatenate(
            [jnp.concatenate([re, im], axis=0) for re, im in pairs], axis=1
        )

    def stages(p):
        col = cols[p]
        off = col % width
        base = pl.multiple_of(col - off, LANES)
        back = (width - off) % width
        first, second = pl.ds(base, width), pl.ds(base + width, width)

        def patch(c):
            a = pltpu.roll(window[c, :, first], back, 1)
            b = pltpu.roll(window[c, :, second], back, 1)
            return jnp.where(lane < width - off, a, b)

        o_re, o_im = patch(0), patch(1)
        waves = []
        for m in range(modes):
            p_re, p_im = probe[0, m, 0], probe[0, m, 1]
            waves.append(
                (
                    (p_re * o_re - p_im * o_im).astype(bf16),
                    (p_re * o_im + p_im * o_re).astype(bf16),
                )
            )
        waves_in = stacked(waves)
        yield
        y = first_product(fl[...], waves_in)
        yield
        spectrum = second_product(y, fr[...])
        yield
        intensity = sum(re * re + im * im for re, im in spectrum)
        scale = measured[0, 0, p] * lax.rsqrt(jnp.maximum(intensity, 0.25))
        corrected = [((re * scale).astype(bf16), (im * scale).astype(bf16)) for re, im in spectrum]
        corrected_in = stacked(corrected)
        yield
        y = first_product(il[...], corrected_in)
        yield
        returned = second_product(y, ir[...])
        yield
        g_re = jnp.zeros((width, width), f32)
        g_im = jnp.zeros((width, width), f32)
        for m in range(modes):
            p_re, p_im = probe[0, m, 0], probe[0, m, 1]
            w_re = waves[m][0].astype(f32) - returned[m][0]
            w_im = waves[m][1].astype(f32) - returned[m][1]
            g_re += p_re * w_re + p_im * w_im
            g_im += p_re * w_im - p_im * w_re
        for c, g in ((0, g_re), (1, g_im)):
            turned = pltpu.roll(g, off, 1)
            grad[c, :, first] += jnp.where(lane >= off, turned, 0.0)
            grad[c, :, second] += jnp.where(lane < off, turned, 0.0)
        yield

    waiting = [stages(p) for p in range(positions)]
    running = []
    while waiting or running:
        if waiting:
            running.append(waiting.pop(0))
        running = [one for one in running if next(one, True) is None]

    for c in range(2):
        upper[0, c] = own[0, c] - step * grad[c, :rows, :columns]
        lower[0, c] = -step * grad[c, rows:, :columns]


def chunk_gradient(cols, object_field, halo, probe, measured, tables, start):
    count = halo.shape[0]
    energies, _, rows, columns = object_field.shape
    modes, _, width, _ = probe.shape[1:]
    positions = measured.shape[2]
    field = jax.ShapeDtypeStruct((count, 2, rows, columns), jnp.float32)
    table = pl.BlockSpec((2 * width, 2 * width), lambda e, c: (0, 0))
    piece = pl.BlockSpec((1, 2, rows, columns), lambda e, c: (e, 0, 0, 0))
    flops = 4 * 2 * (2 * width) * (2 * width) * width * modes * positions * count
    return pl.pallas_call(
        gradient_kernel,
        grid_spec=pltpu.PrefetchScalarGridSpec(
            num_scalar_prefetch=1,
            grid=(count,),
            in_specs=[
                pl.BlockSpec((1, 2, rows, columns), lambda e, c: (e + start, 0, 0, 0)),
                piece,
                pl.BlockSpec((1, modes, 2, width, width), lambda e, c: (e + start, 0, 0, 0, 0)),
                pl.BlockSpec(
                    (1, 1, positions, width, width), lambda e, c: (e + start, 0, 0, 0, 0)
                ),
                table,
                table,
                table,
                table,
            ],
            out_specs=[piece, piece],
            scratch_shapes=[
                pltpu.VMEM((2, width, columns + width), jnp.float32),
                pltpu.VMEM((2, width, columns + width), jnp.float32),
            ],
        ),
        out_shape=[field, field],
        compiler_params=pltpu.CompilerParams(
            dimension_semantics=("arbitrary",), vmem_limit_bytes=40 * 2**20
        ),
        cost_estimate=pl.CostEstimate(
            flops=3 * flops, bytes_accessed=count * 1800000, transcendentals=0
        ),
    )(cols, object_field, halo, probe, measured, *tables)


def solver_kernel(gram, rhs, out):
    size = gram.shape[0]
    g, b = gram[...], rhs[...]
    row = lax.broadcasted_iota(jnp.int32, (size, 1), 0)
    for k in range(size):
        inverse = 1.0 / g[k : k + 1, k : k + 1]
        g_row, b_row = g[k : k + 1] * inverse, b[k : k + 1] * inverse
        column = g[:, k : k + 1]
        g = jnp.where(row == k, g_row, g - column * g_row)
        b = jnp.where(row == k, b_row, b - column * b_row)
    out[...] = b


def energy_sum(total):
    if lax.axis_size("energy") != 2:
        return lax.psum(total, "energy")
    return total + lax.ppermute(total, "energy", [(0, 1), (1, 0)])


def expand_kernel(group, basis, coefficients, out):
    e = pl.program_id(0)
    count, rows, _ = coefficients.shape
    outputs = [(i, c) for i in range(out.shape[0]) for c in range(2)]
    first = e * len(outputs)
    for top in range(0, rows, group):
        totals = [0.0] * len(outputs)
        for k in range(count):
            values = coefficients[k, top : top + group]
            totals = [t + basis[first + j, k] * values for j, t in enumerate(totals)]
        for (i, c), total in zip(outputs, totals):
            out[i, c, top : top + group] = total


def expand(own_basis, coefficients, energies):
    count, rows, columns = coefficients.shape
    block = 2 if energies % 2 == 0 else 1
    group = 16 if rows % 16 == 0 else rows
    return pl.pallas_call(
        functools.partial(expand_kernel, group),
        grid=(energies // block,),
        in_specs=[
            pl.BlockSpec(memory_space=pltpu.SMEM),
            pl.BlockSpec((count, rows, columns), lambda e: (0, 0, 0)),
        ],
        out_specs=pl.BlockSpec((block, 2, rows, columns), lambda e: (e, 0, 0, 0)),
        out_shape=jax.ShapeDtypeStruct((energies, 2, rows, columns), jnp.float32),
        compiler_params=pltpu.CompilerParams(vmem_limit_bytes=24 * 2**20),
    )(own_basis, coefficients)


def build_basis(spectra):
    re, im = spectra[:, 0], spectra[:, 1]
    upper = jnp.stack([re, -im], axis=-1)
    lower = jnp.stack([im, re], axis=-1)
    return jnp.stack([upper, lower], axis=1).reshape(2 * spectra.shape[0], 2 * spectra.shape[2])


def on_device(object_field, probe_modes, measured, scan_cols, spectra, material_order):
    width = probe_modes.shape[-1]
    energies, _, rows, columns = object_field.shape
    materials = spectra.shape[2]
    chunk = energies // CHUNKS if energies % CHUNKS == 0 else energies
    starts = range(0, energies, chunk)
    halos = [shifted(object_field[s : s + chunk], "strip", -1) for s in starts]
    strip_index = lax.axis_index("strip")
    energy_index = lax.axis_index("energy")
    cols = lax.dynamic_index_in_dim(scan_cols, strip_index, 0, keepdims=False)
    tables = (*dft_tables(width, 1), *dft_tables(width, -1))
    basis = build_basis(spectra)
    gram = jnp.dot(basis.T, basis, precision=PRECISE)
    solver_map = pl.pallas_call(
        solver_kernel, out_shape=jax.ShapeDtypeStruct(basis.T.shape, jnp.float32)
    )(gram, basis.T)
    first = energy_index * (2 * energies)
    own_map = lax.dynamic_slice_in_dim(solver_map, first, 2 * energies, axis=1)
    own_basis = lax.dynamic_slice_in_dim(basis, first, 2 * energies, axis=0)
    kept, carried = 0.0, 0.0
    for s, halo in zip(starts, halos):
        upper, lower = chunk_gradient(cols, object_field, halo, probe_modes, measured, tables, s)
        part = own_map[:, 2 * s : 2 * (s + chunk)].reshape(2 * materials, chunk, 2)
        product = functools.partial(jnp.einsum, "kec,ecrx->krx", precision=PRECISE)
        kept += product(part, upper)
        carried += product(part, lower)
    pieces = []
    for top in range(0, rows, rows // 2):
        rows_of = slice(top, top + rows // 2)
        total = kept[:, rows_of] + shifted(carried[:, rows_of], "strip", 1)
        pieces.append(energy_sum(total))
    coefficients = jnp.concatenate(pieces, axis=1)
    estimate = expand(own_basis, coefficients, energies)
    sub_rows = rows // lax.axis_size("energy")
    half = lax.dynamic_slice_in_dim(coefficients, energy_index * sub_rows, sub_rows, axis=1)
    half = half.reshape(materials, 2, 1, sub_rows, columns)
    abundance = jnp.concatenate(
        [
            lax.dynamic_index_in_dim(half, material_order[k], 0, keepdims=True)
            for k in range(materials)
        ],
        axis=0,
    )
    return (estimate, abundance)


def solution(mesh):
    return jax.shard_map(
        on_device,
        mesh=mesh,
        in_specs=(
            P("energy", None, "strip", None),
            P("energy", None, None, None, None),
            P("energy", "strip", None, None, None),
            P(),
            P(),
            P(),
        ),
        out_specs=(P("energy", None, "strip", None), P(None, None, "strip", "energy", None)),
        check_vma=False,
    )
```

```python
import functools

import jax
import jax.numpy as jnp
import ml_dtypes
import numpy as np
from jax import lax
from jax.experimental import pallas as pl
from jax.experimental.pallas import tpu as pltpu
from jax.sharding import PartitionSpec as P

PRECISE = lax.Precision.HIGHEST
CHUNKS = 4
LANES = 128


def shifted(block, axis, distance):
    devices = range(lax.axis_size(axis))
    route = [(i - distance, i) for i in devices if i - distance in devices]
    return lax.ppermute(block, axis, route)


def dft_tables(width, phase_sign):
    counter = np.arange(width)
    angle = (counter[:, None] * counter[None, :] % width) * (2.0 * np.pi / width)
    cosine = (np.cos(angle) / np.sqrt(width)).astype(ml_dtypes.bfloat16)
    sine = (phase_sign * np.sin(angle) / np.sqrt(width)).astype(ml_dtypes.bfloat16)
    left = np.block([[cosine, sine], [-sine, cosine]])
    right = np.block([[cosine, -sine], [sine, cosine]])
    return jnp.asarray(left), jnp.asarray(right)


def gradient_kernel(
    cols, own, halo, probe, measured, fl, fr, il, ir, upper, lower, window, grad
):
    modes, _, width, _ = probe.shape[1:]
    positions = measured.shape[2]
    rows, columns = own.shape[2:]
    f32, bf16 = jnp.float32, jnp.bfloat16
    lane = lax.broadcasted_iota(jnp.int32, (width, width), 1)
    block = own.shape[0]
    window[:, :, :rows, :columns] = own[...]
    window[:, :, rows:, :columns] = halo[...]
    window[:, :, :, columns:] = jnp.zeros((block, 2, width, width), f32)
    grad[...] = jnp.zeros(grad.shape, f32)

    def first_product(left, x):
        y = jnp.dot(left, x, preferred_element_type=f32).astype(bf16)
        return jnp.concatenate(
            [
                jnp.concatenate(
                    [y[:width, m * width : (m + 1) * width], y[width:, m * width : (m + 1) * width]],
                    axis=1,
                )
                for m in range(modes)
            ],
            axis=0,
        )

    def second_product(y, right):
        s = jnp.dot(y, right, preferred_element_type=f32)
        return [
            (s[m * width : (m + 1) * width, :width], s[m * width : (m + 1) * width, width:])
            for m in range(modes)
        ]

    def stacked(pairs):
        return jnp.concatenate(
            [jnp.concatenate([re, im], axis=0) for re, im in pairs], axis=1
        )

    def stages(i, p):
        col = cols[p]
        off = col % width
        base = pl.multiple_of(col - off, LANES)
        back = (width - off) % width
        first, second = pl.ds(base, width), pl.ds(base + width, width)

        def patch(c):
            a = pltpu.roll(window[i, c, :, first], back, 1)
            b = pltpu.roll(window[i, c, :, second], back, 1)
            return jnp.where(lane < width - off, a, b)

        o_re, o_im = patch(0), patch(1)
        waves = []
        for m in range(modes):
            p_re, p_im = probe[i, m, 0], probe[i, m, 1]
            waves.append(
                (
                    (p_re * o_re - p_im * o_im).astype(bf16),
                    (p_re * o_im + p_im * o_re).astype(bf16),
                )
            )
        waves_in = stacked(waves)
        yield
        y = first_product(fl[...], waves_in)
        yield
        spectrum = second_product(y, fr[...])
        yield
        intensity = sum(re * re + im * im for re, im in spectrum)
        scale = measured[i, 0, p] * lax.rsqrt(jnp.maximum(intensity, 0.25))
        corrected = [((re * scale).astype(bf16), (im * scale).astype(bf16)) for re, im in spectrum]
        corrected_in = stacked(corrected)
        yield
        y = first_product(il[...], corrected_in)
        yield
        returned = second_product(y, ir[...])
        yield
        g_re = jnp.zeros((width, width), f32)
        g_im = jnp.zeros((width, width), f32)
        for m in range(modes):
            p_re, p_im = probe[i, m, 0], probe[i, m, 1]
            w_re = waves[m][0].astype(f32) - returned[m][0]
            w_im = waves[m][1].astype(f32) - returned[m][1]
            g_re += p_re * w_re + p_im * w_im
            g_im += p_re * w_im - p_im * w_re
        for c, g in ((0, g_re), (1, g_im)):
            turned = pltpu.roll(g, off, 1)
            grad[i, c, :, first] += jnp.where(lane >= off, turned, 0.0)
            grad[i, c, :, second] += jnp.where(lane < off, turned, 0.0)
        yield

    waiting = [stages(i, p) for i in range(block) for p in range(positions)]
    running = []
    while waiting or running:
        if waiting:
            running.append(waiting.pop(0))
        running = [one for one in running if next(one, True) is None]

    for i in range(block):
        power = jnp.zeros((width, width), f32)
        for m in range(modes):
            p_re, p_im = probe[i, m, 0], probe[i, m, 1]
            power += p_re * p_re + p_im * p_im
        step = 0.5 / jnp.max(jnp.max(power, axis=0, keepdims=True), axis=1, keepdims=True)
        for c in range(2):
            upper[i, c] = own[i, c] - step * grad[i, c, :rows, :columns]
            lower[i, c] = -step * grad[i, c, rows:, :columns]


def chunk_gradient(cols, object_field, halo, probe, measured, tables, start):
    count = halo.shape[0]
    energies, _, rows, columns = object_field.shape
    modes, _, width, _ = probe.shape[1:]
    positions = measured.shape[2]
    field = jax.ShapeDtypeStruct((count, 2, rows, columns), jnp.float32)
    table = pl.BlockSpec((2 * width, 2 * width), lambda e, c: (0, 0))
    block = 2 if count % 2 == 0 and start % 2 == 0 else 1
    skip = start // block
    piece = pl.BlockSpec((block, 2, rows, columns), lambda e, c: (e, 0, 0, 0))
    flops = 4 * 2 * (2 * width) * (2 * width) * width * modes * positions * count
    return pl.pallas_call(
        gradient_kernel,
        grid_spec=pltpu.PrefetchScalarGridSpec(
            num_scalar_prefetch=1,
            grid=(count // block,),
            in_specs=[
                pl.BlockSpec((block, 2, rows, columns), lambda e, c: (e + skip, 0, 0, 0)),
                piece,
                pl.BlockSpec((block, modes, 2, width, width), lambda e, c: (e + skip, 0, 0, 0, 0)),
                pl.BlockSpec(
                    (block, 1, positions, width, width), lambda e, c: (e + skip, 0, 0, 0, 0)
                ),
                table,
                table,
                table,
                table,
            ],
            out_specs=[piece, piece],
            scratch_shapes=[
                pltpu.VMEM((block, 2, width, columns + width), jnp.float32),
                pltpu.VMEM((block, 2, width, columns + width), jnp.float32),
            ],
        ),
        out_shape=[field, field],
        compiler_params=pltpu.CompilerParams(
            dimension_semantics=("arbitrary",), vmem_limit_bytes=40 * 2**20
        ),
        cost_estimate=pl.CostEstimate(
            flops=3 * flops, bytes_accessed=count * 1800000, transcendentals=0
        ),
    )(cols, object_field, halo, probe, measured, *tables)


def solver_kernel(gram, rhs, out):
    size = gram.shape[0]
    g, b = gram[...], rhs[...]
    row = lax.broadcasted_iota(jnp.int32, (size, 1), 0)
    for k in range(size):
        inverse = 1.0 / g[k : k + 1, k : k + 1]
        g_row, b_row = g[k : k + 1] * inverse, b[k : k + 1] * inverse
        column = g[:, k : k + 1]
        g = jnp.where(row == k, g_row, g - column * g_row)
        b = jnp.where(row == k, b_row, b - column * b_row)
    out[...] = b


def energy_sum(total):
    if lax.axis_size("energy") != 2:
        return lax.psum(total, "energy")
    return total + lax.ppermute(total, "energy", [(0, 1), (1, 0)])


def expand_kernel(group, basis, coefficients, out):
    e = pl.program_id(0)
    count, rows, _ = coefficients.shape
    outputs = [(i, c) for i in range(out.shape[0]) for c in range(2)]
    first = e * len(outputs)
    for top in range(0, rows, group):
        totals = [0.0] * len(outputs)
        for k in range(count):
            values = coefficients[k, top : top + group]
            totals = [t + basis[first + j, k] * values for j, t in enumerate(totals)]
        for (i, c), total in zip(outputs, totals):
            out[i, c, top : top + group] = total


def expand(own_basis, coefficients, energies):
    count, rows, columns = coefficients.shape
    block = 2 if energies % 2 == 0 else 1
    group = 16 if rows % 16 == 0 else rows
    return pl.pallas_call(
        functools.partial(expand_kernel, group),
        grid=(energies // block,),
        in_specs=[
            pl.BlockSpec(memory_space=pltpu.SMEM),
            pl.BlockSpec((count, rows, columns), lambda e: (0, 0, 0)),
        ],
        out_specs=pl.BlockSpec((block, 2, rows, columns), lambda e: (e, 0, 0, 0)),
        out_shape=jax.ShapeDtypeStruct((energies, 2, rows, columns), jnp.float32),
        compiler_params=pltpu.CompilerParams(vmem_limit_bytes=24 * 2**20),
    )(own_basis, coefficients)


def build_basis(spectra):
    re, im = spectra[:, 0], spectra[:, 1]
    upper = jnp.stack([re, -im], axis=-1)
    lower = jnp.stack([im, re], axis=-1)
    return jnp.stack([upper, lower], axis=1).reshape(2 * spectra.shape[0], 2 * spectra.shape[2])


def on_device(object_field, probe_modes, measured, scan_cols, spectra, material_order):
    width = probe_modes.shape[-1]
    energies, _, rows, columns = object_field.shape
    materials = spectra.shape[2]
    chunk = energies // CHUNKS if energies % CHUNKS == 0 else energies
    starts = range(0, energies, chunk)
    halos = [shifted(object_field[s : s + chunk], "strip", -1) for s in starts]
    strip_index = lax.axis_index("strip")
    energy_index = lax.axis_index("energy")
    cols = lax.dynamic_index_in_dim(scan_cols, strip_index, 0, keepdims=False)
    tables = (*dft_tables(width, 1), *dft_tables(width, -1))
    basis = build_basis(spectra)
    gram = jnp.dot(basis.T, basis, precision=PRECISE)
    solver_map = pl.pallas_call(
        solver_kernel, out_shape=jax.ShapeDtypeStruct(basis.T.shape, jnp.float32)
    )(gram, basis.T)
    first = energy_index * (2 * energies)
    own_map = lax.dynamic_slice_in_dim(solver_map, first, 2 * energies, axis=1)
    own_basis = lax.dynamic_slice_in_dim(basis, first, 2 * energies, axis=0)
    kept, carried = 0.0, 0.0
    for s, halo in zip(starts, halos):
        upper, lower = chunk_gradient(cols, object_field, halo, probe_modes, measured, tables, s)
        part = own_map[:, 2 * s : 2 * (s + chunk)].reshape(2 * materials, chunk, 2)
        product = functools.partial(jnp.einsum, "kec,ecrx->krx", precision=PRECISE)
        kept += product(part, upper)
        carried += product(part, lower)
    pieces = []
    for top in range(0, rows, rows // 2):
        rows_of = slice(top, top + rows // 2)
        total = kept[:, rows_of] + shifted(carried[:, rows_of], "strip", 1)
        pieces.append(energy_sum(total))
    coefficients = jnp.concatenate(pieces, axis=1)
    estimate = expand(own_basis, coefficients, energies)
    sub_rows = rows // lax.axis_size("energy")
    half = lax.dynamic_slice_in_dim(coefficients, energy_index * sub_rows, sub_rows, axis=1)
    half = half.reshape(materials, 2, 1, sub_rows, columns)
    abundance = jnp.concatenate(
        [
            lax.dynamic_index_in_dim(half, material_order[k], 0, keepdims=True)
            for k in range(materials)
        ],
        axis=0,
    )
    return (estimate, abundance)


def solution(mesh):
    return jax.shard_map(
        on_device,
        mesh=mesh,
        in_specs=(
            P("energy", None, "strip", None),
            P("energy", None, None, None, None),
            P("energy", "strip", None, None, None),
            P(),
            P(),
            P(),
        ),
        out_specs=(P("energy", None, "strip", None), P(None, None, "strip", "energy", None)),
        check_vma=False,
    )
```
